32 devices in a mesh: rows: 4 (over y, x), cols: 8 (over z, core).
Axes of the slice: x: 2, y: 2, z: 4, core: 2. Of those that a mesh axis runs over, the one named last changes fastest.
Arguments:
- ancestor_inv: bfloat16 [4096, 4096], P('rows', 'cols'), may hold values from -0.125 to 0.125
- lfactor: bfloat16 [8, 256, 6, 256], P('cols'), may hold values from -0.8984375 to 0.8984375
- struct: int32 [6, 8], replicated, may hold values from 0 to 15, as said below
- validity: int32 [6, 8], replicated, may hold values from 0 to 1, as said below
- diag_inverse: float32 [6, 256, 256], replicated, may hold values from -6 to 6
Outputs:
- column_block: bfloat16 [4096, 1536], P(('rows', 'cols'))
- diagonal_block: float32 [6, 256, 256], replicated
The draws below stay inside these ranges and needn't reach their ends.
Inputs may be any that keep to these rules, and one draw needn't show every extreme that they name: `struct`: within a supernode the 8 tile indices are distinct and increasing, and every list holds tiles 0 and 15. `validity`: every tile index of 0 to 15 is a valid entry of some supernode's list; some supernode has all 8 flags set.
All inputs are finite; a program needn't handle non-finite values.
Results may differ from the reference program's by a relative error of at most 0.001.
Values may be sent and summed in bfloat16 or wider, within the bound.
A program may use at most 192 MiB of HBM per device.

```python
import jax
import jax.numpy as jnp
from jax import lax

S = 256
SUPER = 6
NT = 16
PAD = 8


def tile_lists_common(key):
    first_key, second_key, third_key = jax.random.split(jax.random.fold_in(key, 7), 3)
    noise_draw = jax.random.randint(first_key, (SUPER, NT), 0, NT)
    indices = jnp.arange(NT, dtype=jnp.int32)
    owners = jnp.arange(SUPER, dtype=jnp.int32)
    forced = (indices[None, :] % SUPER == owners[:, None]) | (indices[None, :] == 0) | (indices[None, :] == NT - 1)
    scores = (noise_draw + indices[None, :]) * NT + indices[None, :]
    scores = jnp.where(forced, 4 * NT * NT + indices[None, :], scores)
    chosen_scores, chosen = lax.top_k(scores, PAD)
    chosen = jnp.sort(chosen, axis=1).astype(jnp.int32)
    owned = chosen % SUPER == owners[:, None]
    coins = jax.random.randint(second_key, (SUPER, PAD), 0, 2)
    filled = jax.random.randint(third_key, (), 0, SUPER)
    full_row = owners[:, None] == filled
    flag_rows = (owned | (coins == 1) | full_row).astype(jnp.int32)
    return (chosen, flag_rows)


def draw_struct(key, part):
    return tile_lists_common(key)[0]


def draw_validity(key, part):
    return tile_lists_common(key)[1]


def block_levels(own_key, shape, shards, least, high):
    def one(dim, blocks):
        heights = jax.random.uniform(jax.random.fold_in(jax.random.fold_in(own_key, 6), dim), (blocks,), jnp.float32, least / len(shards), high / len(shards))
        return jnp.repeat(jnp.exp(heights), shape[dim] // blocks).reshape((-1,) + (1,) * (len(shape) - dim - 1))

    factor_of = one(*shards[0])
    for cut in shards[1:]:
        factor_of = factor_of * one(*cut)
    return factor_of


def gaussian(key, dims, scale, reach, cuts=(), kind=jnp.bfloat16):
    gain = block_levels(key, dims, cuts, -0.22, 0.18) if cuts else 1.0
    drawn = jax.random.normal(key, dims, jnp.float32) * scale * gain
    return jnp.minimum(jnp.maximum(drawn, -reach), reach).astype(kind)


def setup_inputs(seed: int = 0) -> dict:
    splits = jax.random.split(jax.random.key(seed), 6)
    return {
        "ancestor_inv": gaussian(splits[0], (NT * S, NT * S), (PAD * S) ** -0.5, 0.125, ((0, 4), (1, 8))),
        "lfactor": gaussian(splits[1], (PAD, S, SUPER, S), 0.15, 0.8984375, ((0, 8),)),
        "struct": draw_struct(jax.random.fold_in(splits[5], 71), 0),
        "validity": draw_validity(jax.random.fold_in(splits[5], 71), 0),
        "diag_inverse": gaussian(splits[4], (SUPER, S, S), 1.0, 6.0, (), jnp.float32),
    }


def reference(ancestor_inv, lfactor, struct, validity, diag_inverse):
    indices = jnp.arange(NT, dtype=jnp.int32)
    flagged = validity > 0
    selector = ((struct[:, :, None] == indices[None, None, :]) & flagged[:, :, None]).astype(jnp.float32)
    ancestor_panel = jnp.einsum("kpt,pakb->takb", selector, lfactor.astype(jnp.float32), precision=lax.Precision.HIGHEST)
    right_side = ancestor_panel.reshape(NT * S, SUPER * S)
    updates = -jnp.dot(ancestor_inv.astype(jnp.float32), right_side, precision=lax.Precision.HIGHEST)
    row_present = jnp.max(selector, axis=1)
    masked = updates.reshape(NT, S, SUPER, S) * jnp.transpose(row_present)[:, None, :, None]
    column_block = masked.astype(jnp.bfloat16).reshape(NT * S, SUPER * S)
    diagonal_block = diag_inverse - jnp.einsum("akb,akc->kbc", ancestor_panel.reshape(NT * S, SUPER, S), updates.reshape(NT * S, SUPER, S), precision=lax.Precision.HIGHEST)
    return column_block, diagonal_block
```

```python
import functools

import jax
import jax.numpy as jnp
from jax import lax
from jax.experimental import pallas as pl
from jax.experimental.pallas import tpu as pltpu
from jax.sharding import PartitionSpec as P

MESH = pl.DeviceIdType.MESH


def kernel(
    R, C, a_ref, l_ref, struct_ref, valid_ref, d_ref, col_ref, diag_ref,
    abuf, lbuf, q, x1, x2, x3, f,
    loc_sem, a_send, a_recv,
    lz_send_up, lz_send_dn, lz_recv, lp_send, lp_recv, lc_send, lc_recv, lo_send, lo_recv,
    d1_send, d1_recv, d2_send, d2_recv, d3_send, d3_recv,
    d4_send, d4_recv, d5_send, d5_recv, d6_send, d6_recv,
):
    Z = C // 2
    r = lax.axis_index("rows")
    c = lax.axis_index("cols")
    z = c // 2
    core = c % 2
    sib = z * 2 + 1 - core
    E, K, S = l_ref.shape[0], l_ref.shape[1], l_ref.shape[2]
    NP = C * E
    TPD = a_ref.shape[1] // S
    M = a_ref.shape[0] // C
    piece = S // R

    def wrap(v, n):
        return lax.rem(v, n)

    barrier = pltpu.get_barrier_semaphore()
    for d in range(1, C):
        pl.semaphore_signal(barrier, inc=1, device_id=(r, wrap(c + d, C)), device_id_type=MESH)
    for d in range(1, R):
        pl.semaphore_signal(barrier, inc=1, device_id=(wrap(r + d, R), c), device_id_type=MESH)
    pl.semaphore_wait(barrier, C - 1 + R - 1)

    def remote(src, dst, ssem, rsem, dev):
        return pltpu.make_async_remote_copy(
            src_ref=src, dst_ref=dst, send_sem=ssem, recv_sem=rsem,
            device_id=dev, device_id_type=MESH,
        )

    def entry(zz):
        return zz * 2 + core

    def rows_of(rr):
        return pl.ds(pl.multiple_of(rr * piece, piece), piece)

    def own_z(zn, ssem):
        return remote(
            l_ref.at[:, :, rows_of(r), :], lbuf.at[c, :, :, rows_of(r), :],
            ssem, lz_recv.at[z], (r, entry(zn)),
        )

    @pl.when(z + 1 < Z)
    def _():
        own_z(z + 1, lz_send_up.at[z]).start()

    @pl.when(z > 0)
    def _():
        own_z(z - 1, lz_send_dn.at[z]).start()

    own_core = remote(l_ref, lbuf.at[c], lo_send, lo_recv, (r, sib))
    own_core.start()
    own_l = pltpu.make_async_copy(l_ref, lbuf.at[c], loc_sem.at[0])
    own_l.start()

    def a_copy(d, j):
        cn = wrap(c + d, C)
        return remote(
            a_ref.at[pl.ds(pl.multiple_of(cn * M, M), M), pl.ds(j * S, S)],
            abuf.at[c * TPD + j], a_send.at[d, j], a_recv.at[d, j], (r, cn),
        )

    for d in range(1, C):
        for j in range(TPD):
            a_copy(d, j).start()
    own_a = []
    for j in range(TPD):
        own_a.append(pltpu.make_async_copy(
            a_ref.at[pl.ds(pl.multiple_of(c * M, M), M), pl.ds(j * S, S)],
            abuf.at[c * TPD + j], loc_sem.at[1 + j],
        ))
        own_a[-1].start()

    def fwd_z(zz, zn, ssem):
        ref = lbuf.at[entry(zz), :, :, rows_of(r), :]
        return remote(ref, ref, ssem, lz_recv.at[zz], (r, entry(zn)))

    def plane(zz, rr, rn):
        ref = lbuf.at[entry(zz), :, :, rows_of(rr), :]
        return remote(ref, ref, lp_send.at[zz, rn], lp_recv.at[zz, rr], (rn, c))

    def across(zz, rr):
        ref = lbuf.at[entry(zz), :, :, rows_of(rr), :]
        return remote(ref, ref, lc_send.at[zz, rr], lc_recv.at[zz, rr], (r, sib))

    def across_in(zz, rr):
        ref = lbuf.at[zz * 2 + 1 - core, :, :, rows_of(rr), :]
        return remote(ref, ref, lc_send.at[zz, rr], lc_recv.at[zz, rr], (r, sib))

    def arrived(zz):
        for d in range(1, R):
            plane(zz, r, wrap(r + d, R)).start()
        across(zz, r).start()

    for s in range(1, Z):
        @pl.when(z - s >= 0)
        def _():
            fwd_z(z - s, z, lz_send_up.at[z - s]).wait_recv()

            @pl.when(z + 1 < Z)
            def _():
                fwd_z(z - s, z + 1, lz_send_up.at[z - s]).start()
            arrived(z - s)

        @pl.when(z + s < Z)
        def _():
            fwd_z(z + s, z, lz_send_dn.at[z + s]).wait_recv()

            @pl.when(z > 0)
            def _():
                fwd_z(z + s, z - 1, lz_send_dn.at[z + s]).start()
            arrived(z + s)

    for s in range(1, Z):
        zz = wrap(z + s, Z)
        for d in range(1, R):
            rr = wrap(r + d, R)
            plane(zz, rr, r).wait_recv()
            across(zz, rr).start()

    own_l.wait()
    remote(l_ref, lbuf.at[sib], lo_send, lo_recv, (r, sib)).wait_recv()
    for cp in own_a:
        cp.wait()
    for d in range(1, C):
        cs = wrap(c + C - d, C)
        for j in range(TPD):
            remote(
                abuf.at[cs * TPD + j], abuf.at[cs * TPD + j],
                a_send.at[d, j], a_recv.at[d, j], (r, cs),
            ).wait_recv()
    for s in range(1, Z):
        for d in range(R):
            across_in(wrap(z + s, Z), wrap(r + d, R)).wait_recv()

    start_row = r * (C * M) + c * M
    own_tile = start_row // S
    offset = pl.multiple_of(start_row % S, M)

    def one_node(k, carry):
        acc = jnp.zeros((M, S), jnp.float32)
        present = jnp.int32(0)
        which = jnp.int32(0)
        for p in range(NP):
            t = struct_ref[k, p]
            ok = valid_ref[k, p] > 0
            hit = jnp.where(ok & (t == own_tile), 1, 0)
            present = present + hit
            which = which + hit * p
            term = jnp.dot(
                abuf[t], lbuf[p // E, p % E, k], preferred_element_type=jnp.float32
            )
            acc = acc + term * jnp.where(ok, 1.0, 0.0)
        here = present.astype(jnp.float32)
        col_ref[:, pl.ds(pl.multiple_of(k * S, S), S)] = (acc * (-here)).astype(jnp.bfloat16)
        panel = lbuf[which // E, which % E, k, pl.ds(offset, M), :] * here.astype(jnp.bfloat16)
        hi = acc.astype(jnp.bfloat16)
        lo = (acc - hi.astype(jnp.float32)).astype(jnp.bfloat16)
        out = lax.dot_general(
            jnp.concatenate([panel, panel], axis=0), jnp.concatenate([hi, lo], axis=0),
            (((0,), (0,)), ((), ())), preferred_element_type=jnp.float32,
        )
        at = pl.ds(pl.multiple_of(k * S, S), S)
        q[0, at, :] = out[:, : S // 2]
        q[1, at, :] = out[:, S // 2 :]
        return carry

    lax.fori_loop(0, K, one_node, 0)

    n_r = (K * S) // R
    n_z = n_r // Z

    def at_r(rr):
        return pl.ds(pl.multiple_of(rr * n_r, n_r), n_r)

    def at_z(rr, zz):
        return pl.ds(pl.multiple_of(rr * n_r + zz * n_z, n_z), n_z)

    d1 = remote(q.at[1 - core], x1, d1_send, d1_recv, (r, sib))
    d1.start()
    d1.wait_recv()
    x1[...] = x1[...] + q[core]
    d2 = []
    for d in range(1, R):
        rn = wrap(r + d, R)
        d2.append(remote(x1.at[at_r(rn)], x2.at[d - 1], d2_send.at[d - 1], d2_recv.at[d - 1], (rn, c)))
        d2[-1].start()
    part = x1[at_r(r), :]
    for d in range(1, R):
        d2[d - 1].wait_recv()
        part = part + x2[d - 1]
    q[core, at_r(0), :] = part
    d3 = []
    for s in range(1, Z):
        zn = wrap(z + s, Z)
        d3.append(remote(
            q.at[core, at_z(0, zn)], x3.at[s - 1], d3_send.at[s - 1], d3_recv.at[s - 1],
            (r, entry(zn)),
        ))
        d3[-1].start()
    part = q[core, at_z(0, z), :]
    for s in range(1, Z):
        d3[s - 1].wait_recv()
        part = part + x3[s - 1]
    f[core, at_z(r, z), :] = part
    d4 = []
    for s in range(1, Z):
        ref = f.at[core, at_z(r, z)]
        d4.append(remote(ref, ref, d4_send.at[s - 1], d4_recv.at[s - 1], (r, entry(wrap(z + s, Z)))))
        d4[-1].start()
    for s in range(1, Z):
        ref = f.at[core, at_z(r, wrap(z + Z - s, Z))]
        remote(ref, ref, d4_send.at[s - 1], d4_recv.at[s - 1], (r, c)).wait_recv()
    d5 = []
    for d in range(1, R):
        ref = f.at[core, at_r(r)]
        d5.append(remote(ref, ref, d5_send.at[d - 1], d5_recv.at[d - 1], (wrap(r + d, R), c)))
        d5[-1].start()
    d6 = []
    ref = f.at[core, at_r(r)]
    d6.append(remote(ref, ref, d6_send.at[0], d6_recv.at[0], (r, sib)))
    d6[-1].start()
    for d in range(1, R):
        ref = f.at[core, at_r(wrap(r + R - d, R))]
        remote(ref, ref, d5_send.at[d - 1], d5_recv.at[d - 1], (r, c)).wait_recv()
        d6.append(remote(ref, ref, d6_send.at[d], d6_recv.at[d], (r, sib)))
        d6[-1].start()
    for d in range(R):
        ref = f.at[1 - core, at_r(wrap(r + R - d, R))]
        remote(ref, ref, d6_send.at[d], d6_recv.at[d], (r, sib)).wait_recv()
    for k in range(K):
        for h in range(2):
            cut = slice(h * (S // 2), (h + 1) * (S // 2))
            diag_ref[k, :, cut] = d_ref[k, :, cut] + f[h, k * S : (k + 1) * S, :]

    @pl.when(z + 1 < Z)
    def _():
        own_z(z + 1, lz_send_up.at[z]).wait_send()

    @pl.when(z > 0)
    def _():
        own_z(z - 1, lz_send_dn.at[z]).wait_send()

    own_core.wait_send()
    for d in range(1, C):
        for j in range(TPD):
            a_copy(d, j).wait_send()

    def sent(zz):
        for d in range(1, R):
            plane(zz, r, wrap(r + d, R)).wait_send()
        across(zz, r).wait_send()

    for s in range(1, Z):
        @pl.when(z - s >= 0)
        def _():
            @pl.when(z + 1 < Z)
            def _():
                fwd_z(z - s, z + 1, lz_send_up.at[z - s]).wait_send()
            sent(z - s)

        @pl.when(z + s < Z)
        def _():
            @pl.when(z > 0)
            def _():
                fwd_z(z + s, z - 1, lz_send_dn.at[z + s]).wait_send()
            sent(z + s)

    for s in range(1, Z):
        zz = wrap(z + s, Z)
        for d in range(1, R):
            across(zz, wrap(r + d, R)).wait_send()
    for cp in [d1] + d2 + d3 + d4 + d5 + d6:
        cp.wait_send()


def body(R, C, ancestor_inv, lfactor, struct, validity, diag_inverse):
    E, S, K, _ = lfactor.shape
    Z = C // 2
    rows, width = ancestor_inv.shape
    M = rows // C
    TPD = width // S
    NT = C * TPD
    tall = K * S
    half = S // 2
    factor = jnp.transpose(lfactor, (0, 2, 1, 3))
    dma = pltpu.SemaphoreType.DMA
    column_block, diagonal = pl.pallas_call(
        functools.partial(kernel, R, C),
        out_shape=(
            jax.ShapeDtypeStruct((M, K * S), jnp.bfloat16),
            jax.ShapeDtypeStruct((K, S, S), jnp.float32),
        ),
        in_specs=[
            pl.BlockSpec(memory_space=pl.ANY),
            pl.BlockSpec(memory_space=pl.ANY),
            pl.BlockSpec(memory_space=pltpu.SMEM),
            pl.BlockSpec(memory_space=pltpu.SMEM),
            pl.BlockSpec(memory_space=pltpu.VMEM),
        ],
        out_specs=(
            pl.BlockSpec(memory_space=pltpu.VMEM),
            pl.BlockSpec(memory_space=pltpu.VMEM),
        ),
        scratch_shapes=[
            pltpu.VMEM((NT, M, S), jnp.bfloat16),
            pltpu.VMEM((C, E, K, S, S), jnp.bfloat16),
            pltpu.VMEM((2, tall, half), jnp.float32),
            pltpu.VMEM((tall, half), jnp.float32),
            pltpu.VMEM((R - 1, tall // R, half), jnp.float32),
            pltpu.VMEM((Z - 1, tall // R // Z, half), jnp.float32),
            pltpu.VMEM((2, tall, half), jnp.float32),
            dma((1 + TPD,)), dma((C, TPD)), dma((C, TPD)),
            dma((Z,)), dma((Z,)), dma((Z,)),
            dma((Z, R)), dma((Z, R)), dma((Z, R)), dma((Z, R)), dma, dma,
            dma, dma, dma((R - 1,)), dma((R - 1,)), dma((Z - 1,)), dma((Z - 1,)),
            dma((Z - 1,)), dma((Z - 1,)), dma((R - 1,)), dma((R - 1,)), dma((R,)), dma((R,)),
        ],
        compiler_params=pltpu.CompilerParams(
            collective_id=0, has_side_effects=True, vmem_limit_bytes=56 * 1024 * 1024
        ),
    )(ancestor_inv, factor, struct, validity, diag_inverse)
    return column_block, diagonal


def solution(mesh):
    return jax.shard_map(
        functools.partial(body, mesh.shape["rows"], mesh.shape["cols"]),
        mesh=mesh,
        in_specs=(P("rows", "cols"), P("cols", None, None, None), P(), P(), P()),
        out_specs=(P(("rows", "cols"), None), P()),
        check_vma=False,
    )
```

```python
import functools

import jax
import jax.numpy as jnp
from jax import lax
from jax.experimental import pallas as pl
from jax.experimental.pallas import tpu as pltpu
from jax.sharding import PartitionSpec as P

MESH = pl.DeviceIdType.MESH
GROUPS = 3


def kernel(
    R, C, a_ref, l_ref, struct_ref, valid_ref, col_ref, f,
    abuf, tiles, lbuf, q, x1, x2, x3,
    loc_sem, a_send, a_recv,
    lz_send_up, lz_send_dn, lz_recv, lp_send, lp_recv, lh_send, lh_recv, lc_send, lc_recv, lo_send, lo_recv,
    d1_send, d1_recv, d2_send, d2_recv, d3_send, d3_recv,
    d4_send, d4_recv, d5_send, d5_recv, d6_send, d6_recv,
):
    Z = C // 2
    r = lax.axis_index("rows")
    c = lax.axis_index("cols")
    z = c // 2
    core = c % 2
    sib = z * 2 + 1 - core
    E, K, S = l_ref.shape[0], l_ref.shape[1], l_ref.shape[2]
    NP = C * E
    TPD = a_ref.shape[1] // S
    M = a_ref.shape[0] // C
    piece = S // R
    G = q.shape[1]
    KG = K // G

    def wrap(v, n):
        return lax.rem(v, n)

    barrier = pltpu.get_barrier_semaphore()
    for d in range(1, C):
        pl.semaphore_signal(barrier, inc=1, device_id=(r, wrap(c + d, C)), device_id_type=MESH)
    for d in range(1, R):
        pl.semaphore_signal(barrier, inc=1, device_id=(wrap(r + d, R), c), device_id_type=MESH)
    pl.semaphore_wait(barrier, C - 1 + R - 1)

    def remote(src, dst, ssem, rsem, dev):
        return pltpu.make_async_remote_copy(
            src_ref=src, dst_ref=dst, send_sem=ssem, recv_sem=rsem,
            device_id=dev, device_id_type=MESH,
        )

    def entry(zz):
        return zz * 2 + core

    def rows_of(rr):
        return pl.ds(pl.multiple_of(rr * piece, piece), piece)

    def own_z(zn, ssem):
        return remote(
            l_ref.at[:, :, rows_of(r), :], lbuf.at[c, :, :, rows_of(r), :],
            ssem, lz_recv.at[z], (r, entry(zn)),
        )

    @pl.when(z + 1 < Z)
    def _():
        own_z(z + 1, lz_send_up.at[z]).start()

    @pl.when(z > 0)
    def _():
        own_z(z - 1, lz_send_dn.at[z]).start()

    own_core = remote(l_ref, lbuf.at[c], lo_send, lo_recv, (r, sib))
    own_core.start()
    own_l = pltpu.make_async_copy(l_ref, lbuf.at[c], loc_sem.at[0])
    own_l.start()

    def a_copy(d):
        cn = wrap(c + d, C)
        return remote(
            a_ref.at[pl.ds(pl.multiple_of(cn * M, M), M), :],
            abuf.at[c], a_send.at[d], a_recv.at[d], (r, cn),
        )

    own_a = pltpu.make_async_copy(
        a_ref.at[pl.ds(pl.multiple_of(c * M, M), M), :], abuf.at[c], loc_sem.at[1]
    )
    own_a.start()

    def fwd_z(zz, zn, ssem):
        ref = lbuf.at[entry(zz), :, :, rows_of(r), :]
        return remote(ref, ref, ssem, lz_recv.at[zz], (r, entry(zn)))

    def plane(zz, rr, rn):
        ref = lbuf.at[entry(zz), :, :, rows_of(rr), :]
        return remote(ref, ref, lp_send.at[zz, rn], lp_recv.at[zz, rr], (rn, c))

    def across(zz, rr):
        ref = lbuf.at[entry(zz), :, :, rows_of(rr), :]
        return remote(ref, ref, lc_send.at[zz, rr], lc_recv.at[zz, rr], (r, sib))

    def across_in(zz, rr):
        ref = lbuf.at[zz * 2 + 1 - core, :, :, rows_of(rr), :]
        return remote(ref, ref, lc_send.at[zz, rr], lc_recv.at[zz, rr], (r, sib))

    square = R == 4
    near = [r + 1 - 2 * lax.rem(r, 2), wrap(r + 2, R)] if square else []
    part_rows = piece // 2

    def half_ref(zz, rr, h):
        at = pl.ds(pl.multiple_of(rr * piece + h * part_rows, part_rows), part_rows)
        return lbuf.at[entry(zz), :, :, at, :]

    def corner(zz, rr, h, rn):
        ref = half_ref(zz, rr, h)
        return remote(ref, ref, lh_send.at[zz, h], lh_recv.at[zz, h], (rn, c))

    targets = near if square else [wrap(r + d, R) for d in range(1, R)]

    def arrived(zz):
        for rn in targets:
            plane(zz, r, rn).start()
        across(zz, r).start()

    def send_slabs():
        for d in sorted(range(1, C), key=lambda d: abs(d - C // 2)):
            a_copy(d).start()

    for s in range(1, Z):
        if s == Z - 1:
            send_slabs()
        @pl.when(z - s >= 0)
        def _():
            fwd_z(z - s, z, lz_send_up.at[z - s]).wait_recv()

            @pl.when(z + 1 < Z)
            def _():
                fwd_z(z - s, z + 1, lz_send_up.at[z - s]).start()
            arrived(z - s)

        @pl.when(z + s < Z)
        def _():
            fwd_z(z + s, z, lz_send_dn.at[z + s]).wait_recv()

            @pl.when(z > 0)
            def _():
                fwd_z(z + s, z - 1, lz_send_dn.at[z + s]).start()
            arrived(z + s)

    for s in range(1, Z):
        zz = wrap(z + s, Z)
        for i, rr in enumerate(targets):
            plane(zz, rr, r).wait_recv()
            if square:
                corner(zz, rr, i, near[1 - i]).start()
            across(zz, rr).start()
    if square:
        far = near[0] + near[1] - r
        for s in range(1, Z):
            zz = wrap(z + s, Z)
            for h in range(2):
                corner(zz, far, h, r).wait_recv()
            across(zz, far).start()

    own_l.wait()
    remote(l_ref, lbuf.at[sib], lo_send, lo_recv, (r, sib)).wait_recv()
    def cut_tiles(cs):
        for j in range(TPD):
            tiles[cs * TPD + j] = abuf[cs, :, j * S : (j + 1) * S]

    own_a.wait()
    cut_tiles(c)
    for d in range(1, C):
        cs = wrap(c + C - d, C)
        remote(abuf.at[cs], abuf.at[cs], a_send.at[d], a_recv.at[d], (r, cs)).wait_recv()
        cut_tiles(cs)
    for s in range(1, Z):
        for d in range(R):
            across_in(wrap(z + s, Z), wrap(r + d, R)).wait_recv()

    start_row = r * (C * M) + c * M
    own_tile = start_row // S
    offset = pl.multiple_of(start_row % S, M)

    def one_node(g, k, carry):
        acc = jnp.zeros((M, S), jnp.float32)
        present = jnp.int32(0)
        which = jnp.int32(0)
        for p in range(NP):
            t = struct_ref[k, p]
            ok = valid_ref[k, p] > 0
            hit = jnp.where(ok & (t == own_tile), 1, 0)
            present = present + hit
            which = which + hit * p
            term = jnp.dot(
                tiles[t],
                lbuf[p // E, p % E, k],
                preferred_element_type=jnp.float32,
            )
            acc = acc + term * jnp.where(ok, 1.0, 0.0)
        here = present.astype(jnp.float32)
        col_ref[:, pl.ds(pl.multiple_of(k * S, S), S)] = (acc * (-here)).astype(jnp.bfloat16)
        panel = lbuf[which // E, which % E, k, pl.ds(offset, M), :] * here.astype(jnp.bfloat16)
        hi = acc.astype(jnp.bfloat16)
        lo = (acc - hi.astype(jnp.float32)).astype(jnp.bfloat16)
        out = lax.dot_general(
            jnp.concatenate([panel, panel], axis=0), jnp.concatenate([hi, lo], axis=0),
            (((0,), (0,)), ((), ())), preferred_element_type=jnp.float32,
        )
        at = pl.ds(pl.multiple_of((k - g * KG) * S, S), S)
        q[0, g, at, :] = out[:, : S // 2]
        q[1, g, at, :] = out[:, S // 2 :]
        return carry

    n_r = (KG * S) // R
    n_z = n_r // Z
    sends = []

    def at_r(rr):
        return pl.ds(pl.multiple_of(rr * n_r, n_r), n_r)

    def at_z(rr, zz):
        return pl.ds(pl.multiple_of(rr * n_r + zz * n_z, n_z), n_z)

    def launch(*args):
        cp = remote(*args)
        cp.start()
        sends.append(cp)

    def landed(ref, ssem, rsem):
        remote(ref, ref, ssem, rsem, (r, sib)).wait_recv()

    def multiply(g):
        lax.fori_loop(g * KG, (g + 1) * KG, functools.partial(one_node, g), 0)
        launch(q.at[1 - core, g], x1.at[g], d1_send.at[g], d1_recv.at[g], (r, sib))

    def add_core(g):
        landed(x1.at[g], d1_send.at[g], d1_recv.at[g])
        x1[g] = x1[g] + q[core, g]
        for d in range(1, R):
            rn = wrap(r + d, R)
            launch(
                x1.at[g, at_r(rn)], x2.at[g, d - 1],
                d2_send.at[g, d - 1], d2_recv.at[g, d - 1], (rn, c),
            )

    def add_plane(g):
        part = x1[g, at_r(r), :]
        for d in range(1, R):
            landed(x2.at[g, d - 1], d2_send.at[g, d - 1], d2_recv.at[g, d - 1])
            part = part + x2[g, d - 1]
        q[core, g, at_r(0), :] = part
        for s in range(1, Z):
            zn = wrap(z + s, Z)
            launch(
                q.at[core, g, at_z(0, zn)], x3.at[g, s - 1],
                d3_send.at[g, s - 1], d3_recv.at[g, s - 1], (r, entry(zn)),
            )

    def add_z(g):
        part = q[core, g, at_z(0, z), :]
        for s in range(1, Z):
            landed(x3.at[g, s - 1], d3_send.at[g, s - 1], d3_recv.at[g, s - 1])
            part = part + x3[g, s - 1]
        f[core, g, at_z(r, z), :] = part
        ref = f.at[core, g, at_z(r, z)]
        for s in range(1, Z):
            launch(
                ref, ref, d4_send.at[g, s - 1], d4_recv.at[g, s - 1],
                (r, entry(wrap(z + s, Z))),
            )

    def spread_plane(g):
        for s in range(1, Z):
            ref = f.at[core, g, at_z(r, wrap(z + Z - s, Z))]
            landed(ref, d4_send.at[g, s - 1], d4_recv.at[g, s - 1])
        ref = f.at[core, g, at_r(r)]
        for d in range(1, R):
            launch(
                ref, ref, d5_send.at[g, d - 1], d5_recv.at[g, d - 1], (wrap(r + d, R), c)
            )
        launch(ref, ref, d6_send.at[g, 0], d6_recv.at[g, 0], (r, sib))

    def spread_core(g):
        for d in range(1, R):
            ref = f.at[core, g, at_r(wrap(r + R - d, R))]
            landed(ref, d5_send.at[g, d - 1], d5_recv.at[g, d - 1])
            launch(ref, ref, d6_send.at[g, d], d6_recv.at[g, d], (r, sib))

    def store(g):
        for d in range(R):
            ref = f.at[1 - core, g, at_r(wrap(r + R - d, R))]
            landed(ref, d6_send.at[g, d], d6_recv.at[g, d])

    stages = [multiply, add_core, add_plane, add_z, spread_plane, spread_core, store]
    for step in range(len(stages) + G - 1):
        for g in range(G):
            if 0 <= step - g < len(stages):
                stages[step - g](g)

    @pl.when(z + 1 < Z)
    def _():
        own_z(z + 1, lz_send_up.at[z]).wait_send()

    @pl.when(z > 0)
    def _():
        own_z(z - 1, lz_send_dn.at[z]).wait_send()

    own_core.wait_send()
    for d in range(1, C):
        a_copy(d).wait_send()

    def sent(zz):
        for rn in targets:
            plane(zz, r, rn).wait_send()
        across(zz, r).wait_send()

    for s in range(1, Z):
        @pl.when(z - s >= 0)
        def _():
            @pl.when(z + 1 < Z)
            def _():
                fwd_z(z - s, z + 1, lz_send_up.at[z - s]).wait_send()
            sent(z - s)

        @pl.when(z + s < Z)
        def _():
            @pl.when(z > 0)
            def _():
                fwd_z(z + s, z - 1, lz_send_dn.at[z + s]).wait_send()
            sent(z + s)

    for s in range(1, Z):
        zz = wrap(z + s, Z)
        for d in range(1, R):
            across(zz, wrap(r + d, R)).wait_send()
        if square:
            for h in range(2):
                corner(zz, near[h], h, near[1 - h]).wait_send()
    for cp in sends:
        cp.wait_send()


def body(R, C, ancestor_inv, lfactor, struct, validity, diag_inverse):
    E, S, K, _ = lfactor.shape
    Z = C // 2
    rows, width = ancestor_inv.shape
    M = rows // C
    G = GROUPS if K % GROUPS == 0 else 1
    tall = K // G * S
    half = S // 2
    factor = jnp.transpose(lfactor, (0, 2, 1, 3))
    dma = pltpu.SemaphoreType.DMA
    column_block, sums = pl.pallas_call(
        functools.partial(kernel, R, C),
        out_shape=(
            jax.ShapeDtypeStruct((M, K * S), jnp.bfloat16),
            jax.ShapeDtypeStruct((2, G, tall, half), jnp.float32),
        ),
        in_specs=[
            pl.BlockSpec(memory_space=pl.ANY),
            pl.BlockSpec(memory_space=pl.ANY),
            pl.BlockSpec(memory_space=pltpu.SMEM),
            pl.BlockSpec(memory_space=pltpu.SMEM),
        ],
        out_specs=(
            pl.BlockSpec(memory_space=pltpu.VMEM),
            pl.BlockSpec(memory_space=pltpu.VMEM),
        ),
        scratch_shapes=[
            pltpu.VMEM((C, M, width), jnp.bfloat16),
            pltpu.VMEM((C * (width // S), M, S), jnp.bfloat16),
            pltpu.VMEM((C, E, K, S, S), jnp.bfloat16),
            pltpu.VMEM((2, G, tall, half), jnp.float32),
            pltpu.VMEM((G, tall, half), jnp.float32),
            pltpu.VMEM((G, R - 1, tall // R, half), jnp.float32),
            pltpu.VMEM((G, Z - 1, tall // R // Z, half), jnp.float32),
            dma((2,)), dma((C,)), dma((C,)),
            dma((Z,)), dma((Z,)), dma((Z,)),
            dma((Z, R)), dma((Z, R)), dma((Z, 2)), dma((Z, 2)), dma((Z, R)), dma((Z, R)), dma, dma,
            dma((G,)), dma((G,)), dma((G, R - 1)), dma((G, R - 1)), dma((G, Z - 1)), dma((G, Z - 1)),
            dma((G, Z - 1)), dma((G, Z - 1)), dma((G, R - 1)), dma((G, R - 1)), dma((G, R)), dma((G, R)),
        ],
        compiler_params=pltpu.CompilerParams(
            collective_id=0, has_side_effects=True, vmem_limit_bytes=56 * 1024 * 1024
        ),
    )(ancestor_inv, factor, struct, validity)
    sums = jnp.concatenate([sums[0], sums[1]], axis=-1).reshape(K, S, S)
    return column_block, diag_inverse + sums


def solution(mesh):
    return jax.shard_map(
        functools.partial(body, mesh.shape["rows"], mesh.shape["cols"]),
        mesh=mesh,
        in_specs=(P("rows", "cols"), P("cols", None, None, None), P(), P(), P()),
        out_specs=(P(("rows", "cols"), None), P()),
        check_vma=False,
    )
```
